32 devices in a mesh: blk: 8 (over z, x), rep: 4 (over y, core).
Axes of the slice: x: 2, y: 2, z: 4, core: 2. Of those that a mesh axis runs over, the one named last changes fastest.
Arguments:
- features: bfloat16 [8192, 128], P('blk'), may hold values from -6 to 6
- weight: bfloat16 [128, 128], replicated, may hold values from -0.5 to 0.5
- bias: float32 [128], replicated, may hold values from -3 to 3
- tiles: bfloat16 [8, 4, 8, 4, 128, 128], P('blk', 'rep'), may hold values from -0.1875 to 0.1875
- tile_row: int32 [8, 4, 8, 4], P('blk', 'rep'), may hold values from 0 to 7
- tile_col: int32 [8, 4, 8, 4], P('blk', 'rep'), may hold values from 0 to 7
- tile_live: int32 [8, 4, 8], P('blk', 'rep'), may hold values from 1 to 4, as said below
- label_mask: int32 [8192], P(('blk', 'rep')), may hold values 0 or 1
- cotangent: bfloat16 [8192, 128], P(('blk', 'rep')), may hold values from -6 to 6
Outputs:
- output: bfloat16 [8192, 128], P(('blk', 'rep'))
- grad_weight: float32 [128, 128], replicated
- grad_bias: float32 [128], replicated
The draws below stay inside these ranges and needn't reach their ends.
Inputs may be any that keep to these rules, and one draw needn't show every extreme that they name: `tile_live`: some entry equals 4 and some equals 1.
All inputs are finite; a program needn't handle non-finite values. No bound on the sum of `label_mask` on one device may be relied on, other than what follows from the above.
Results may differ from the reference program's by a relative error of at most 0.0056.
Values may be sent and summed in bfloat16 or wider, within the bound.
No kernel may reach another device: no remote copies, remote signals or barrier semaphores. Data moves between devices by JAX's collectives and lax.ppermute only.
A program may use at most 64 MiB of HBM per device.

```python
import jax
import jax.numpy as jnp
from jax import lax

FEAT = 128
HID = 128
TILE = 128
SLOTS = 4
RBLK = 8
NODES = 8192
N_BLK = 8
N_REP = 4


def draw_tile_live(key, part):
    counts = jax.random.randint(key, (N_BLK, N_REP, N_BLK), 1, SLOTS + 1).astype(jnp.int32)
    counts = counts.at[0, 0, 0].set(SLOTS)
    return counts.at[0, 0, 1].set(1)


def with_ends(entries, stream_key, low, top_value):
    longest = entries.shape.index(max(entries.shape))
    spots = []
    for shift in (0, 1):
        where = [jax.random.randint(jax.random.fold_in(stream_key, axis), (), 0, length) for axis, length in enumerate(entries.shape)]
        where[longest] = (where[longest] + shift) % entries.shape[longest]
        spots.append(tuple(where))
    return entries.at[spots[0]].set(low).at[spots[1]].set(top_value)


def shard_levels(rng, extent, split, low, high):
    def one(position, parts):
        steps = jax.random.uniform(jax.random.fold_in(jax.random.fold_in(rng, 6), position), (parts,), jnp.float32, low / len(split), high / len(split))
        return jnp.repeat(jnp.exp(steps), extent[position] // parts).reshape((-1,) + (1,) * (len(extent) - position - 1))

    factor_of = one(*split[0])
    for cut in split[1:]:
        factor_of = factor_of * one(*cut)
    return factor_of


def noise(key, extent, spread, limit, split=(), held_as=jnp.bfloat16):
    drawn = spread * jax.random.normal(key, extent, jnp.float32)
    if split:
        drawn = drawn * shard_levels(key, extent, split, -0.22, 0.18)
    return jnp.clip(drawn, -limit, limit).astype(held_as)


def setup_inputs(seed: int = 0) -> dict:
    arg_keys = jax.random.split(jax.random.key(seed), 10)
    features = noise(arg_keys[0], (NODES, FEAT), 1.0, 6.0, ((0, 8),))
    weight = noise(arg_keys[1], (FEAT, HID), FEAT ** -0.5, 0.5)
    bias = noise(arg_keys[2], (HID,), 0.5, 3.0, (), jnp.float32)
    tiles = noise(arg_keys[3], (N_BLK, N_REP, N_BLK, SLOTS, TILE, TILE), (TILE * N_BLK * N_REP * SLOTS // (2 * RBLK)) ** -0.5, 0.1875, ((0, 8), (1, 4)))
    tile_row = with_ends(jax.random.randint(arg_keys[4], (N_BLK, N_REP, N_BLK, SLOTS), 0, RBLK), jax.random.fold_in(arg_keys[4], 1), 0, RBLK - 1).astype(jnp.int32)
    tile_col = with_ends(jax.random.randint(arg_keys[5], (N_BLK, N_REP, N_BLK, SLOTS), 0, RBLK), jax.random.fold_in(arg_keys[5], 1), 0, RBLK - 1).astype(jnp.int32)
    tile_live = draw_tile_live(jax.random.fold_in(arg_keys[9], 71), 0)
    label_mask = with_ends((jax.random.randint(arg_keys[7], (NODES,), 0, 2) < 1).astype(jnp.int32), jax.random.fold_in(arg_keys[7], 1), 0, 1)
    cotangent = noise(arg_keys[8], (NODES, HID), 1.0, 6.0, ((0, 32),))
    return {"features": features, "weight": weight, "bias": bias, "tiles": tiles, "tile_row": tile_row, "tile_col": tile_col, "tile_live": tile_live, "label_mask": label_mask, "cotangent": cotangent}


def shard_term(block_feat, values, rows_idx, cols_idx, count):
    blocks = block_feat.shape[0] // TILE
    stacked = block_feat.reshape(blocks, TILE, FEAT)
    picked = jnp.take(stacked, cols_idx, axis=0).astype(jnp.float32)
    prod = jnp.einsum("kij,kjf->kif", values.astype(jnp.float32), picked, precision=lax.Precision.HIGHEST)
    alive = jnp.arange(SLOTS, dtype=jnp.int32) < count
    chosen = (rows_idx[None, :] == jnp.arange(blocks, dtype=jnp.int32)[:, None]) & alive[None, :]
    onehot = jnp.where(chosen, 1.0, 0.0).astype(jnp.float32)
    summed = jnp.einsum("rk,kif->rif", onehot, prod, precision=lax.Precision.HIGHEST)
    return summed.reshape(blocks * TILE, FEAT)


def reference(features, weight, bias, tiles, tile_row, tile_col, tile_live, label_mask, cotangent):
    shard_rows = RBLK * TILE
    shards = features.reshape(N_BLK, shard_rows, FEAT)

    def one_shard(owner):
        def add(total, column):
            block = shards[column]
            for part in range(N_REP):
                total = total + shard_term(block, tiles[owner, part, column], tile_row[owner, part, column], tile_col[owner, part, column], tile_live[owner, part, column])
            return total, None

        start = jnp.zeros((shard_rows, FEAT), jnp.float32)
        total, _ = lax.scan(add, start, jnp.arange(N_BLK, dtype=jnp.int32))
        return total

    aggregated = lax.map(one_shard, jnp.arange(N_BLK, dtype=jnp.int32)).reshape(N_BLK * shard_rows, FEAT)
    agg_rounded = aggregated.astype(jnp.bfloat16)
    pre = jnp.dot(agg_rounded, weight, preferred_element_type=jnp.float32) + bias[None, :]
    sigma = jax.nn.sigmoid(pre)
    output = (pre * sigma).astype(jnp.bfloat16)
    slope = sigma * (1.0 + pre * (1.0 - sigma))
    delta = cotangent.astype(jnp.float32) * label_mask.astype(jnp.float32)[:, None] * slope
    delta_rounded = delta.astype(jnp.bfloat16)
    grad_weight = jnp.dot(agg_rounded.T, delta_rounded, preferred_element_type=jnp.float32)
    grad_bias = jnp.sum(delta, axis=0)
    return output, grad_weight, grad_bias
```

```python
import functools

import jax
import jax.numpy as jnp
from jax import lax
from jax.experimental import pallas as pl
from jax.experimental.pallas import tpu as pltpu
from jax.sharding import PartitionSpec as P

VMEM = pl.BlockSpec(memory_space=pltpu.VMEM)
SMEM = pl.BlockSpec(memory_space=pltpu.SMEM)
LIMIT = 48 * 1024 * 1024


def spmm_kernel(nblk, nrep, *refs):
    rows_ref, cols_ref, live_ref, tiles_ref, own_ref = refs[:5]
    near = refs[5 : 5 + nblk - 1]
    far = refs[5 + nblk - 1 : 5 + 2 * (nblk - 1)]
    mine_ref, keep_ref, send_ref, feat, acc = refs[5 + 2 * (nblk - 1) :]
    me = lax.axis_index("blk")
    rep = lax.axis_index("rep")
    core, pair = rep % 2, rep // 2
    npair = nrep // 2
    slots, tile = tiles_ref.shape[1], tiles_ref.shape[2]
    rblk = own_ref.shape[0] // tile
    half = rblk // 2

    acc[...] = jnp.zeros_like(acc)
    feat[0] = own_ref[...].reshape(feat.shape[1:])
    for s in range(1, nblk):
        feat[s, pl.ds(core * half, half)] = near[s - 1][...].reshape((half,) + feat.shape[2:])
        feat[s, pl.ds((1 - core) * half, half)] = far[s - 1][...].reshape((half,) + feat.shape[2:])

    def shard_step(s):
        shard = (me - s + nblk) % nblk
        for k in range(slots):
            prod = jnp.dot(tiles_ref[shard, k], feat[s, cols_ref[shard, k]], preferred_element_type=jnp.float32)
            row = jnp.where(k < live_ref[shard], rows_ref[shard, k], rblk)
            at = pl.ds(pl.multiple_of(row * tile, tile), tile)
            acc[at] = acc[at] + prod

    if nblk <= 8:
        for s in range(nblk):
            shard_step(s)
    else:
        lax.fori_loop(0, nblk, lambda s, c: (shard_step(s), c)[1], 0)

    share = rblk * tile // nrep

    def part(owner):
        return acc[pl.ds(pl.multiple_of(owner * share, share), share)]

    for s in range(npair):
        other = (pair + s) % npair
        send_ref[s] = part(2 * other + 1 - core)
        if s == 0:
            mine_ref[...] = part(2 * other + core)
        else:
            keep_ref[s - 1] = part(2 * other + core)


def tail_kernel(npieces, mine_ref, first_ref, got_ref, weight_ref, bias_ref, cot_ref, out_ref, grad_ref):
    agg = mine_ref[...] + first_ref[0]
    for i in range(got_ref.shape[0]):
        agg = agg + got_ref[i]
    agg = agg.astype(jnp.bfloat16)
    pre = jnp.dot(agg, weight_ref[...], preferred_element_type=jnp.float32) + bias_ref[...]
    sigma = 1.0 / (1.0 + jnp.exp(-pre))
    out_ref[...] = (pre * sigma).astype(jnp.bfloat16)
    delta = cot_ref[...].astype(jnp.float32) * (sigma * (1.0 + pre * (1.0 - sigma)))
    gw = lax.dot_general(
        agg, delta.astype(jnp.bfloat16), (((0,), (0,)), ((), ())), preferred_element_type=jnp.float32
    )
    gb = jnp.sum(delta, axis=0, keepdims=True)
    feat = gw.shape[0]
    grad_ref[pl.ds(0, feat)] = gw
    grad_ref[pl.ds(feat, grad_ref.shape[0] - feat)] = jnp.zeros(
        (grad_ref.shape[0] - feat, gw.shape[1]), jnp.float32
    )
    grad_ref[pl.ds(feat, 1)] = gb


def shards(features, weight, bias, tiles, tile_row, tile_col, tile_live, label_mask, cotangent):
    nblk, nrep = lax.axis_size("blk"), lax.axis_size("rep")
    npair = nrep // 2
    rep = lax.axis_index("rep")
    core = rep % 2
    local, feat_dim = features.shape
    tile = tiles.shape[-1]
    rblk = local // tile
    half = local // 2
    hid = weight.shape[1]
    share = local // nrep
    swap = [(i, i ^ 1) for i in range(nrep)]

    half_own = lax.dynamic_slice_in_dim(features, core * half, half, 0)
    near, far = [], []
    for s in range(1, nblk):
        got = lax.ppermute(half_own, "blk", [(i, (i + s) % nblk) for i in range(nblk)])
        near.append(got)
        far.append(lax.ppermute(got, "rep", swap))

    masked = cotangent * label_mask.astype(jnp.bfloat16)[:, None]

    mine, keep, send = pl.pallas_call(
        functools.partial(spmm_kernel, nblk, nrep),
        out_shape=(
            jax.ShapeDtypeStruct((share, feat_dim), jnp.float32),
            jax.ShapeDtypeStruct((npair - 1, share, feat_dim), jnp.float32),
            jax.ShapeDtypeStruct((npair, share, feat_dim), jnp.float32),
        ),
        in_specs=[SMEM] * 3 + [VMEM] * (2 + 2 * (nblk - 1)),
        out_specs=(VMEM,) * 3,
        scratch_shapes=[
            pltpu.VMEM((nblk, rblk, tile, feat_dim), jnp.bfloat16),
            pltpu.VMEM(((rblk + 1) * tile, feat_dim), jnp.float32),
        ],
        compiler_params=pltpu.CompilerParams(vmem_limit_bytes=LIMIT),
    )(tile_row[0, 0], tile_col[0, 0], tile_live[0, 0], tiles[0, 0], features, *near, *far)

    first = lax.ppermute(send, "rep", swap)
    across = keep + first[1:]
    got = []
    for s in range(1, npair):
        got.append(
            lax.ppermute(across[s - 1], "rep", [(i, (i + 2 * s) % nrep) for i in range(nrep)])
        )
    got = jnp.stack(got)

    ndev = nblk * nrep
    piece = 8 * -(-(feat_dim + 1) // (8 * ndev))
    output, grads = pl.pallas_call(
        functools.partial(tail_kernel, ndev),
        out_shape=(
            jax.ShapeDtypeStruct((share, hid), jnp.bfloat16),
            jax.ShapeDtypeStruct((ndev * piece, hid), jnp.float32),
        ),
        in_specs=[VMEM] * 6,
        out_specs=(VMEM,) * 2,
        compiler_params=pltpu.CompilerParams(vmem_limit_bytes=LIMIT),
    )(mine, first, got, weight, bias[None, :], masked)

    both = ("blk", "rep")
    pieces = lax.all_to_all(grads.reshape(ndev, piece, hid), both, 0, 0)
    total = jnp.sum(pieces, axis=0)
    spread = lax.all_to_all(jnp.broadcast_to(total[None], (ndev, piece, hid)), both, 0, 0)
    spread = spread.reshape(ndev * piece, hid)
    return output, spread[:feat_dim], spread[feat_dim]


def solution(mesh):
    placed = (
        P("blk", None),
        P(),
        P(),
        P("blk", "rep", None, None, None, None),
        P("blk", "rep", None, None),
        P("blk", "rep", None, None),
        P("blk", "rep", None),
        P(("blk", "rep")),
        P(("blk", "rep"), None),
    )
    return jax.shard_map(
        shards,
        mesh=mesh,
        in_specs=placed,
        out_specs=(P(("blk", "rep"), None), P(), P()),
        check_vma=False,
    )
```

```python
import functools

import jax
import jax.numpy as jnp
from jax import lax
from jax.experimental import pallas as pl
from jax.experimental.pallas import tpu as pltpu
from jax.sharding import PartitionSpec as P

VMEM = pl.BlockSpec(memory_space=pltpu.VMEM)
SMEM = pl.BlockSpec(memory_space=pltpu.SMEM)
HBM = pl.BlockSpec(memory_space=pltpu.HBM)
ANY = pl.BlockSpec(memory_space=pl.ANY)
LIMIT = 48 * 1024 * 1024
BOTH = ("blk", "rep")


def stage_kernel(rblk, *refs):
    sources, targets = refs[:9], refs[9:13] + refs[15:20]
    masked_ref, code_ref, sems = refs[13], refs[14], refs[20]
    mask_ref, cot_ref, row_ref, col_ref, live_ref = targets[4:]
    copies = [pltpu.make_async_copy(x, y, sems.at[i]) for i, (x, y) in enumerate(zip(sources, targets))]
    for copy in reversed(copies):
        copy.start()
    for copy in copies[4:]:
        copy.wait()
    share = cot_ref.shape[0]
    eye = lax.broadcasted_iota(jnp.int32, (share, share), 0) == lax.broadcasted_iota(jnp.int32, (share, share), 1)
    column = jnp.sum(jnp.where(eye, mask_ref[...].astype(jnp.float32), 0.0), axis=1, keepdims=True)
    masked_ref[...] = (cot_ref[...].astype(jnp.float32) * column).astype(jnp.bfloat16)
    slot = lax.broadcasted_iota(jnp.int32, code_ref.shape, 0)
    row = jnp.where(slot < live_ref[0], row_ref[0, 0], rblk)
    code_ref[...] = row * rblk + col_ref[0, 0]
    for copy in copies[:4]:
        copy.wait()


def spmm_kernel(nblk, nrep, plan, *refs):
    code_ref, tiles_ref = refs[:2]
    pieces = refs[2 : 2 + len(plan)]
    keep_ref, send_ref, feat, acc = refs[3 + len(plan) :]
    me = lax.axis_index("blk")
    core = lax.axis_index("rep") % 2
    npair = nrep // 2
    slots, tile = tiles_ref.shape[3], tiles_ref.shape[4]
    rblk = feat.shape[1]

    acc[...] = jnp.zeros_like(acc)
    for ref, (off0, off1, rows) in zip(pieces, plan):
        off = jnp.where(core == 0, off0, off1)
        if rows is None:
            feat[off] = ref[...].reshape(feat.shape[1:])
        else:
            half = rblk // 2
            at = jnp.where(core == 0, rows[0], rows[1]) * half
            feat[off, pl.ds(at, half)] = ref[...].reshape((half,) + feat.shape[2:])

    def shard_step(off):
        shard = jnp.bitwise_xor(me, off)
        for k in range(slots):
            code = code_ref[k, shard]
            row, col = code // rblk, code % rblk
            prod = jnp.dot(tiles_ref[0, 0, shard, k], feat[off, col], preferred_element_type=jnp.float32)
            at = pl.ds(pl.multiple_of(row * tile, tile), tile)
            acc[at] = acc[at] + prod

    if nblk <= 8:
        for off in range(nblk):
            shard_step(off)
    else:
        lax.fori_loop(0, nblk, lambda s, c: (shard_step(s), c)[1], 0)

    share = rblk * tile // nrep

    def part(owner):
        return acc[pl.ds(pl.multiple_of(owner * share, share), share)]

    for p in range(npair):
        keep_ref[pl.ds(p * share, share)] = part(2 * p + core)
        send_ref[pl.ds(p * share, share)] = part(2 * p + 1 - core)


def tail_kernel(*refs):
    mine_ref, got_ref = refs[:2]
    weight_ref, bias_ref, cot_ref, out_ref, grad_ref, act = refs[2:]
    share = out_ref.shape[0]
    agg = (mine_ref[...] + got_ref[...]).astype(jnp.bfloat16)
    pre = jnp.dot(agg, weight_ref[...], preferred_element_type=jnp.float32) + bias_ref[...]
    sigma = 1.0 / (1.0 + jnp.exp(-pre))
    act[...] = pre * sigma
    pair = lax.axis_index("rep") // 2
    out_ref[...] = act[pl.ds(pl.multiple_of(pair * share, share), share)].astype(jnp.bfloat16)
    delta = cot_ref[...].astype(jnp.float32) * (sigma * (1.0 + pre * (1.0 - sigma)))
    gw = lax.dot_general(
        agg, delta.astype(jnp.bfloat16), (((0,), (0,)), ((), ())), preferred_element_type=jnp.float32
    )
    gb = jnp.sum(delta, axis=0, keepdims=True)
    feat = gw.shape[0]
    grad_ref[pl.ds(0, feat)] = gw
    grad_ref[pl.ds(feat, 8)] = jnp.broadcast_to(gb, (8, gb.shape[1]))


def last_kernel(a_ref, b_ref, gw_ref, gb_ref):
    feat = gw_ref.shape[0]
    total = a_ref[...] + b_ref[...]
    gw_ref[...] = total[:feat]
    gb_ref[...] = total[feat : feat + 1]


def fence_kernel(x_ref, *refs):
    refs[-1][...] = x_ref[...]


def fence(x, *others):
    return pl.pallas_call(
        fence_kernel,
        out_shape=jax.ShapeDtypeStruct(x.shape, x.dtype),
        in_specs=[VMEM] + [ANY] * len(others),
        out_specs=VMEM,
        compiler_params=params(),
    )(x, *others)


def params():
    return pltpu.CompilerParams(vmem_limit_bytes=LIMIT)


def shards(features, weight, bias, tiles, tile_row, tile_col, tile_live, label_mask, cotangent):
    nblk, nrep = lax.axis_size("blk"), lax.axis_size("rep")
    npair = nrep // 2
    rep = lax.axis_index("rep")
    core = rep % 2
    local, feat_dim = features.shape
    tile = tiles.shape[-1]
    rblk = local // tile
    half = local // 2
    hid = weight.shape[1]
    share = local // nrep

    def blk_swap(x, off):
        return lax.ppermute(x, "blk", [(i, i ^ off) for i in range(nblk)])

    def rep_swap(x, off):
        return lax.ppermute(x, "rep", [(i, i ^ off) for i in range(nrep)])

    def two_ways(x, off0, off1):
        return lax.ppermute(
            x,
            BOTH,
            [(b * nrep + r, (b ^ (off1 if r % 2 else off0)) * nrep + r) for b in range(nblk) for r in range(nrep)],
        )

    arrays, plan = [], []

    def add(array, off0, off1, rows=None):
        arrays.append(array)
        plan.append((off0, off1, rows))

    def stage():
        return pl.pallas_call(
            functools.partial(stage_kernel, rblk),
            out_shape=(
                jax.ShapeDtypeStruct(tiles.shape, tiles.dtype),
                jax.ShapeDtypeStruct(features.shape, features.dtype),
                jax.ShapeDtypeStruct(weight.shape, weight.dtype),
                jax.ShapeDtypeStruct((1, hid), bias.dtype),
                jax.ShapeDtypeStruct(cotangent.shape, cotangent.dtype),
                jax.ShapeDtypeStruct((tile_row.shape[3], tile_row.shape[2]), jnp.int32),
            ),
            in_specs=[HBM] * 9,
            out_specs=(VMEM,) * 6,
            scratch_shapes=[
                pltpu.VMEM((1, share), label_mask.dtype),
                pltpu.VMEM(cotangent.shape, cotangent.dtype),
                pltpu.VMEM((1, 1, tile_row.shape[3], tile_row.shape[2]), jnp.int32),
                pltpu.VMEM((1, 1, tile_row.shape[3], tile_row.shape[2]), jnp.int32),
                pltpu.VMEM(tile_live.shape, jnp.int32),
                pltpu.SemaphoreType.DMA((9,)),
            ],
            compiler_params=params(),
            cost_estimate=pl.CostEstimate(flops=0, bytes_accessed=2 * tiles.size * 2, transcendentals=0),
        )(
            tiles,
            features,
            weight,
            bias[None, :],
            label_mask[None, :],
            cotangent,
            jnp.swapaxes(tile_row, 2, 3),
            jnp.swapaxes(tile_col, 2, 3),
            tile_live,
        )

    known = [(features, 0)]
    far = nblk // 2
    while far > 4:
        known += [(blk_swap(x, far), off ^ far) for x, off in known]
        far //= 2
    for own, base in known:
        second = two_ways(own, 2, 3)
        first = two_ways(own, 4, 1)
        if base == 0:
            tiles_v, own, weight_v, bias_v, masked, code = stage()
            first = fence(first, second, masked)
        first_x = rep_swap(first, 1)
        across = jnp.where(core == 0, first, first_x)
        third = two_ways(across, 1, 2)
        fourth = blk_swap(lax.dynamic_slice_in_dim(across, core * half, half, 0), 3)
        add(own, base, base)
        second_x = rep_swap(second, 1)
        third_x = rep_swap(third, 1)
        fourth_x = rep_swap(fourth, 1)
        add(first, base ^ 4, base ^ 1)
        add(first_x, base ^ 1, base ^ 4)
        add(second, base ^ 2, base ^ 3)
        add(second_x, base ^ 3, base ^ 2)
        add(third, base ^ 5, base ^ 6)
        add(third_x, base ^ 6, base ^ 5)
        add(fourth, base ^ 7, base ^ 7, (0, 1))
        add(fourth_x, base ^ 7, base ^ 7, (1, 0))

    cots = [(masked, 0)]
    for i in range(1, npair):
        cots.append((rep_swap(masked, 2 * i), i))
    if npair == 2:
        mine, other = cots[0][0], cots[1][0]
        low = rep // 2 == 0
        cot = jnp.concatenate([jnp.where(low, mine, other), jnp.where(low, other, mine)], axis=0)
    else:
        stacked = jnp.stack([x for x, _ in cots])
        order = jnp.arange(npair, dtype=jnp.int32) ^ (rep // 2)
        cot = jnp.take(stacked, order, axis=0).reshape(npair * share, hid)

    keep, send = pl.pallas_call(
        functools.partial(spmm_kernel, nblk, nrep, tuple(plan)),
        out_shape=(jax.ShapeDtypeStruct((npair * share, feat_dim), jnp.float32),) * 2,
        in_specs=[SMEM] + [VMEM] * (1 + len(arrays)) + [ANY],
        out_specs=(VMEM,) * 2,
        scratch_shapes=[
            pltpu.VMEM((nblk, rblk, tile, feat_dim), jnp.bfloat16),
            pltpu.VMEM(((rblk + 1) * tile, feat_dim), jnp.float32),
        ],
        compiler_params=params(),
    )(code, tiles_v, *arrays, cot)

    total, got = keep, rep_swap(send, 1)
    bit = 1
    while bit < npair:
        total = total + got
        got = rep_swap(total, 2 * bit)
        bit *= 2

    output, grads = pl.pallas_call(
        tail_kernel,
        out_shape=(
            jax.ShapeDtypeStruct((share, hid), jnp.bfloat16),
            jax.ShapeDtypeStruct((feat_dim + 8, hid), jnp.float32),
        ),
        in_specs=[VMEM] * 5,
        out_specs=(VMEM,) * 2,
        scratch_shapes=[pltpu.VMEM((npair * share, hid), jnp.float32)],
        compiler_params=params(),
    )(total, got, weight_v, bias_v, cot)

    got = rep_swap(grads, 1)
    bit = 1
    while bit < nblk:
        grads = grads + got
        got = blk_swap(grads, bit)
        bit *= 2
    grad_weight, grad_bias = pl.pallas_call(
        last_kernel,
        out_shape=(
            jax.ShapeDtypeStruct((feat_dim, hid), jnp.float32),
            jax.ShapeDtypeStruct((1, hid), jnp.float32),
        ),
        in_specs=[VMEM] * 2,
        out_specs=(VMEM,) * 2,
        compiler_params=params(),
    )(grads, got)
    return output, grad_weight, grad_bias.reshape(hid)


def solution(mesh):
    placed = (
        P("blk", None),
        P(),
        P(),
        P("blk", "rep", None, None, None, None),
        P("blk", "rep", None, None),
        P("blk", "rep", None, None),
        P("blk", "rep", None),
        P(BOTH),
        P(BOTH, None),
    )
    return jax.shard_map(
        shards,
        mesh=mesh,
        in_specs=placed,
        out_specs=(P(BOTH, None), P(), P()),
        check_vma=False,
    )
```

```python
import functools

import jax
import jax.numpy as jnp
from jax import lax
from jax.experimental import pallas as pl
from jax.experimental.pallas import tpu as pltpu
from jax.sharding import PartitionSpec as P

VMEM = pl.BlockSpec(memory_space=pltpu.VMEM)
SMEM = pl.BlockSpec(memory_space=pltpu.SMEM)
HBM = pl.BlockSpec(memory_space=pltpu.HBM)
ANY = pl.BlockSpec(memory_space=pl.ANY)
LIMIT = 48 * 1024 * 1024
BOTH = ("blk", "rep")


def stage_kernel(rblk, *refs):
    sources, targets = refs[:9], refs[9:13] + refs[15:20]
    masked_ref, code_ref, sems = refs[13], refs[14], refs[20]
    mask_ref, cot_ref, row_ref, col_ref, live_ref = targets[4:]
    copies = [pltpu.make_async_copy(x, y, sems.at[i]) for i, (x, y) in enumerate(zip(sources, targets))]
    for copy in reversed(copies):
        copy.start()
    for copy in copies[4:]:
        copy.wait()
    share = cot_ref.shape[0]
    eye = lax.broadcasted_iota(jnp.int32, (share, share), 0) == lax.broadcasted_iota(jnp.int32, (share, share), 1)
    column = jnp.sum(jnp.where(eye, mask_ref[...].astype(jnp.float32), 0.0), axis=1, keepdims=True)
    masked_ref[...] = (cot_ref[...].astype(jnp.float32) * column).astype(jnp.bfloat16)
    slot = lax.broadcasted_iota(jnp.int32, code_ref.shape, 0)
    row = jnp.where(slot < live_ref[0], row_ref[0, 0], rblk)
    code_ref[...] = row * rblk + col_ref[0, 0]
    for copy in copies[:4]:
        copy.wait()


def spmm_kernel(nblk, nrep, plan, *refs):
    code_ref, tiles_ref = refs[:2]
    pieces = refs[2 : 2 + len(plan)]
    keep_ref, send_ref, feat, acc = refs[3 + len(plan) :]
    me = lax.axis_index("blk")
    core = lax.axis_index("rep") % 2
    npair = nrep // 2
    slots, tile = tiles_ref.shape[3], tiles_ref.shape[4]
    rblk = feat.shape[1]

    acc[...] = jnp.zeros_like(acc)
    for ref, (off0, off1) in zip(pieces, plan):
        feat[jnp.where(core == 0, off0, off1)] = ref[...].reshape(feat.shape[1:])

    def shard_step(off):
        shard = jnp.bitwise_xor(me, off)
        for k in range(slots):
            code = code_ref[k, shard]
            row, col = code // rblk, code % rblk
            prod = jnp.dot(tiles_ref[0, 0, shard, k], feat[off, col], preferred_element_type=jnp.float32)
            at = pl.ds(pl.multiple_of(row * tile, tile), tile)
            acc[at] = acc[at] + prod

    if nblk <= 8:
        for off in range(nblk):
            shard_step(off)
    else:
        lax.fori_loop(0, nblk, lambda s, c: (shard_step(s), c)[1], 0)

    share = rblk * tile // nrep

    def part(owner):
        return acc[pl.ds(pl.multiple_of(owner * share, share), share)]

    for p in range(npair):
        keep_ref[pl.ds(p * share, share)] = part(2 * p + core)
        send_ref[pl.ds(p * share, share)] = part(2 * p + 1 - core)


def tail_kernel(*refs):
    agg_ref, weight_ref, bias_ref, cot_ref, out_ref, keep_ref, send_ref, act, grad = refs
    share = out_ref.shape[0]
    agg = agg_ref[...]
    pre = jnp.dot(agg, weight_ref[...], preferred_element_type=jnp.float32) + bias_ref[...]
    sigma = 1.0 / (1.0 + jnp.exp(-pre))
    act[...] = pre * sigma
    pair = lax.axis_index("rep") // 2
    out_ref[...] = act[pl.ds(pl.multiple_of(pair * share, share), share)].astype(jnp.bfloat16)
    delta = cot_ref[...].astype(jnp.float32) * (sigma * (1.0 + pre * (1.0 - sigma)))
    gw = lax.dot_general(
        agg, delta.astype(jnp.bfloat16), (((0,), (0,)), ((), ())), preferred_element_type=jnp.float32
    )
    gb = jnp.sum(delta, axis=0, keepdims=True)
    half = gw.shape[0] // 2
    core = lax.axis_index("rep") % 2
    grad[...] = gw
    for ref, which in ((keep_ref, core), (send_ref, 1 - core)):
        ref[pl.ds(0, half)] = grad[pl.ds(pl.multiple_of(which * half, half), half)]
        ref[pl.ds(half, 8)] = jnp.broadcast_to(gb, (8, gb.shape[1]))


def last_kernel(mine_ref, other_ref, gw_ref, gb_ref):
    half = gw_ref.shape[0] // 2
    core = lax.axis_index("rep") % 2
    gw_ref[pl.ds(pl.multiple_of(core * half, half), half)] = mine_ref[pl.ds(0, half)]
    gw_ref[pl.ds(pl.multiple_of((1 - core) * half, half), half)] = other_ref[pl.ds(0, half)]
    gb_ref[...] = mine_ref[pl.ds(half, 1)]


def fence_kernel(x_ref, *refs):
    refs[-1][...] = x_ref[...]


def fence(x, *others):
    return pl.pallas_call(
        fence_kernel,
        out_shape=jax.ShapeDtypeStruct(x.shape, x.dtype),
        in_specs=[VMEM] + [ANY] * len(others),
        out_specs=VMEM,
        compiler_params=params(),
    )(x, *others)


def params():
    return pltpu.CompilerParams(vmem_limit_bytes=LIMIT)


def shards(features, weight, bias, tiles, tile_row, tile_col, tile_live, label_mask, cotangent):
    nblk, nrep = lax.axis_size("blk"), lax.axis_size("rep")
    npair = nrep // 2
    rep = lax.axis_index("rep")
    core = rep % 2
    side = (rep // 2) % 2
    local, feat_dim = features.shape
    tile = tiles.shape[-1]
    rblk = local // tile
    half = local // 2
    hid = weight.shape[1]
    share = local // nrep

    def blk_swap(x, off):
        return lax.ppermute(x, "blk", [(i, i ^ off) for i in range(nblk)])

    def rep_swap(x, off):
        return lax.ppermute(x, "rep", [(i, i ^ off) for i in range(nrep)])

    def two_ways(x, off0, off1):
        return lax.ppermute(
            x,
            BOTH,
            [(b * nrep + r, (b ^ (off1 if r % 2 else off0)) * nrep + r) for b in range(nblk) for r in range(nrep)],
        )

    def one_core(x, axis, off, which):
        if axis == "blk":
            return lax.ppermute(
                x, BOTH, [(b * nrep + r, (b ^ off) * nrep + r) for b in range(nblk) for r in range(which, nrep, 2)]
            )
        return lax.ppermute(x, "rep", [(r, r ^ off) for r in range(which, nrep, 2)])

    arrays, plan = [], []

    def add(array, off0, off1):
        arrays.append(array)
        plan.append((off0, off1))

    def stage():
        return pl.pallas_call(
            functools.partial(stage_kernel, rblk),
            out_shape=(
                jax.ShapeDtypeStruct(tiles.shape, tiles.dtype),
                jax.ShapeDtypeStruct(features.shape, features.dtype),
                jax.ShapeDtypeStruct(weight.shape, weight.dtype),
                jax.ShapeDtypeStruct((1, hid), bias.dtype),
                jax.ShapeDtypeStruct(cotangent.shape, cotangent.dtype),
                jax.ShapeDtypeStruct((tile_row.shape[3], tile_row.shape[2]), jnp.int32),
            ),
            in_specs=[HBM] * 9,
            out_specs=(VMEM,) * 6,
            scratch_shapes=[
                pltpu.VMEM((1, share), label_mask.dtype),
                pltpu.VMEM(cotangent.shape, cotangent.dtype),
                pltpu.VMEM((1, 1, tile_row.shape[3], tile_row.shape[2]), jnp.int32),
                pltpu.VMEM((1, 1, tile_row.shape[3], tile_row.shape[2]), jnp.int32),
                pltpu.VMEM(tile_live.shape, jnp.int32),
                pltpu.SemaphoreType.DMA((9,)),
            ],
            compiler_params=params(),
            cost_estimate=pl.CostEstimate(flops=0, bytes_accessed=2 * tiles.size * 2, transcendentals=0),
        )(
            tiles,
            features,
            weight,
            bias[None, :],
            label_mask[None, :],
            cotangent,
            jnp.swapaxes(tile_row, 2, 3),
            jnp.swapaxes(tile_col, 2, 3),
            tile_live,
        )

    known = [(features, 0)]
    far = nblk // 2
    while far > 4:
        known += [(blk_swap(x, far), off ^ far) for x, off in known]
        far //= 2
    for own, base in known:
        first = two_ways(own, 4, 1)
        own_half = lax.dynamic_slice_in_dim(own, side * half, half, 0)
        second = two_ways(own_half, 3, 2)
        packed = second
        if base == 0:
            tiles_v, own, weight_v, bias_v, masked, code = stage()
            first = fence(first, second, masked)
            packed = jnp.concatenate([second, masked], axis=0)
        first_x = rep_swap(first, 1)
        third = one_core(first, "blk", 3, 0)
        across = jnp.where(core == 0, first, first_x)
        fourth = two_ways(across, 2, 1)
        packed_y = rep_swap(fence(packed, across), 2)
        if base == 0:
            other = packed_y[half:]
        second_y = packed_y[:half]
        low = side == 0
        near = jnp.concatenate([jnp.where(low, second, second_y), jnp.where(low, second_y, second)], axis=0)
        near_x = rep_swap(near, 1)
        third_x = one_core(third, "rep", 1, 0)
        fourth_x = rep_swap(fourth, 1)
        add(own, base, base)
        add(first, base ^ 4, base ^ 1)
        add(first_x, base ^ 1, base ^ 4)
        add(near, base ^ 3, base ^ 2)
        add(near_x, base ^ 2, base ^ 3)
        add(jnp.where(core == 0, third, third_x), base ^ 7, base ^ 7)
        add(fourth, base ^ 6, base ^ 5)
        add(fourth_x, base ^ 5, base ^ 6)

    if npair == 2:
        cot = jnp.concatenate([jnp.where(side == 0, masked, other), jnp.where(side == 0, other, masked)], axis=0)
    else:
        stacked = jnp.stack([masked] + [rep_swap(masked, 2 * i) for i in range(1, npair)])
        order = jnp.arange(npair, dtype=jnp.int32) ^ (rep // 2)
        cot = jnp.take(stacked, order, axis=0).reshape(npair * share, hid)

    keep, send = pl.pallas_call(
        functools.partial(spmm_kernel, nblk, nrep, tuple(plan)),
        out_shape=(jax.ShapeDtypeStruct((npair * share, feat_dim), jnp.float32),) * 2,
        in_specs=[SMEM] + [VMEM] * (1 + len(arrays)) + [ANY],
        out_specs=(VMEM,) * 2,
        scratch_shapes=[
            pltpu.VMEM((nblk, rblk, tile, feat_dim), jnp.bfloat16),
            pltpu.VMEM(((rblk + 1) * tile, feat_dim), jnp.float32),
        ],
        compiler_params=params(),
    )(code, tiles_v, *arrays, cot)

    total, got = keep, rep_swap(send, 1)
    total = total + got
    if npair == 2:
        sent = lax.optimization_barrier((4.0 * total).astype(jnp.float16))
        total = sent.astype(jnp.float32) + rep_swap(sent, 2).astype(jnp.float32)
        total = (0.25 * total).astype(jnp.bfloat16)
    else:
        bit = 1
        while bit < npair:
            total = total + rep_swap(total, 2 * bit)
            bit *= 2
        total = total.astype(jnp.bfloat16)

    output, grads, send = pl.pallas_call(
        tail_kernel,
        out_shape=(
            jax.ShapeDtypeStruct((share, hid), jnp.bfloat16),
            jax.ShapeDtypeStruct((feat_dim // 2 + 8, hid), jnp.float32),
            jax.ShapeDtypeStruct((feat_dim // 2 + 8, hid), jnp.float32),
        ),
        in_specs=[VMEM] * 4,
        out_specs=(VMEM,) * 3,
        scratch_shapes=[
            pltpu.VMEM((npair * share, hid), jnp.float32),
            pltpu.VMEM((feat_dim, hid), jnp.float32),
        ],
        compiler_params=params(),
    )(total, weight_v, bias_v, cot)

    grads = grads + rep_swap(send, 1)
    bit = 1
    while bit < nblk:
        grads = grads + blk_swap(grads, bit)
        bit *= 2
    grad_weight, grad_bias = pl.pallas_call(
        last_kernel,
        out_shape=(
            jax.ShapeDtypeStruct((feat_dim, hid), jnp.float32),
            jax.ShapeDtypeStruct((1, hid), jnp.float32),
        ),
        in_specs=[VMEM] * 2,
        out_specs=(VMEM,) * 2,
        compiler_params=params(),
    )(grads, rep_swap(grads, 1))
    return output, grad_weight, grad_bias.reshape(hid)


def solution(mesh):
    placed = (
        P("blk", None),
        P(),
        P(),
        P("blk", "rep", None, None, None, None),
        P("blk", "rep", None, None),
        P("blk", "rep", None, None),
        P("blk", "rep", None),
        P(BOTH),
        P(BOTH, None),
    )
    return jax.shard_map(
        shards,
        mesh=mesh,
        in_specs=placed,
        out_specs=(P(BOTH, None), P(), P()),
        check_vma=False,
    )
```

```python
import functools

import jax
import jax.numpy as jnp
from jax import lax
from jax.experimental import pallas as pl
from jax.experimental.pallas import tpu as pltpu
from jax.sharding import PartitionSpec as P

VMEM = pl.BlockSpec(memory_space=pltpu.VMEM)
SMEM = pl.BlockSpec(memory_space=pltpu.SMEM)
HBM = pl.BlockSpec(memory_space=pltpu.HBM)
ANY = pl.BlockSpec(memory_space=pl.ANY)
LIMIT = 48 * 1024 * 1024
BOTH = ("blk", "rep")


def shard_of(which, plan, j):
    return jnp.bitwise_xor(lax.axis_index("blk"), jnp.where(which == 0, plan[j][0], plan[j][1]))


def stage_kernel(rblk, plan, *refs):
    tiles_in, keep_ref, send_ref = refs[0], refs[8], refs[9]
    sources, targets = refs[1:8], refs[10:12] + refs[14:19]
    masked_ref, code_ref, tile_sems, sems = refs[12], refs[13], refs[19], refs[20]
    mask_ref, cot_ref, row_ref, col_ref, live_ref = targets[2:]
    copies = [pltpu.make_async_copy(x, y, sems.at[i]) for i, (x, y) in enumerate(zip(sources, targets))]
    core = lax.axis_index("rep") % 2
    for j in range(len(plan)):
        for i, (which, ref) in enumerate(((core, keep_ref), (1 - core, send_ref))):
            shard = shard_of(which, plan, j)
            copies.append(pltpu.make_async_copy(tiles_in.at[0, 0, shard], ref.at[j], tile_sems.at[2 * j + i]))
    for copy in copies:
        copy.start()
    for copy in copies[2:7]:
        copy.wait()
    share = cot_ref.shape[0]
    eye = lax.broadcasted_iota(jnp.int32, (share, share), 0) == lax.broadcasted_iota(jnp.int32, (share, share), 1)
    column = jnp.sum(jnp.where(eye, mask_ref[...].astype(jnp.float32), 0.0), axis=1, keepdims=True)
    masked_ref[...] = (cot_ref[...].astype(jnp.float32) * column).astype(jnp.bfloat16)
    slot = lax.broadcasted_iota(jnp.int32, code_ref.shape, 0)
    row = jnp.where(slot < live_ref[0], row_ref[0, 0], rblk)
    code_ref[...] = row * rblk + col_ref[0, 0]
    for copy in copies[:2] + copies[7:]:
        copy.wait()


def spmm_kernel(nrep, rblk, plan, *refs):
    codes, tiles = refs[:2], refs[2:4]
    pieces = refs[4 : 4 + len(plan)]
    keep_ref, send_ref, acc = refs[5 + len(plan) :]
    core = lax.axis_index("rep") % 2
    npair = nrep // 2
    slots, tile = tiles[0].shape[1], tiles[0].shape[2]

    acc[...] = jnp.zeros_like(acc)
    for j, piece in enumerate(pieces):
        shard = shard_of(core, plan, j)
        for code_ref, tiles_ref in zip(codes, tiles):
            for k in range(slots):
                code = code_ref[k, shard]
                row, col = code // rblk, code % rblk
                block = piece[pl.ds(pl.multiple_of(col * tile, tile), tile)]
                prod = jnp.dot(tiles_ref[j, k], block, preferred_element_type=jnp.float32)
                at = pl.ds(pl.multiple_of(row * tile, tile), tile)
                acc[at] = acc[at] + prod

    share = rblk * tile // nrep

    def part(owner):
        return acc[pl.ds(pl.multiple_of(owner * share, share), share)]

    for p in range(npair):
        keep_ref[pl.ds(p * share, share)] = part(2 * p + core)
        send_ref[pl.ds(p * share, share)] = part(2 * p + 1 - core)


def tail_kernel(*refs):
    agg_ref, weight_ref, bias_ref, cot_ref, act_ref, keep_ref, send_ref, grad = refs
    agg = agg_ref[...]
    pre = jnp.dot(agg, weight_ref[...], preferred_element_type=jnp.float32) + bias_ref[...]
    sigma = 1.0 / (1.0 + jnp.exp(-pre))
    act_ref[...] = pre * sigma
    delta = cot_ref[...].astype(jnp.float32) * (sigma * (1.0 + pre * (1.0 - sigma)))
    gw = lax.dot_general(
        agg, delta.astype(jnp.bfloat16), (((0,), (0,)), ((), ())), preferred_element_type=jnp.float32
    )
    gb = jnp.sum(delta, axis=0, keepdims=True)
    half = gw.shape[0] // 2
    core = lax.axis_index("rep") % 2
    grad[...] = gw
    for ref, which in ((keep_ref, core), (send_ref, 1 - core)):
        ref[pl.ds(0, half)] = grad[pl.ds(pl.multiple_of(which * half, half), half)]
        ref[pl.ds(half, 8)] = jnp.broadcast_to(gb, (8, gb.shape[1]))


def last_kernel(mine_ref, other_ref, gw_ref, gb_ref):
    half = gw_ref.shape[0] // 2
    core = lax.axis_index("rep") % 2
    gw_ref[pl.ds(pl.multiple_of(core * half, half), half)] = mine_ref[pl.ds(0, half)]
    gw_ref[pl.ds(pl.multiple_of((1 - core) * half, half), half)] = other_ref[pl.ds(0, half)]
    gb_ref[...] = mine_ref[pl.ds(half, 1)]


def fence_kernel(x_ref, *refs):
    refs[-1][...] = x_ref[...]


def fence(x, *others):
    return pl.pallas_call(
        fence_kernel,
        out_shape=jax.ShapeDtypeStruct(x.shape, x.dtype),
        in_specs=[VMEM] + [ANY] * len(others),
        out_specs=VMEM,
        compiler_params=params(),
    )(x, *others)


def params():
    return pltpu.CompilerParams(vmem_limit_bytes=LIMIT)


def shards(features, weight, bias, tiles, tile_row, tile_col, tile_live, label_mask, cotangent):
    nblk, nrep = lax.axis_size("blk"), lax.axis_size("rep")
    npair = nrep // 2
    rep = lax.axis_index("rep")
    core = rep % 2
    side = (rep // 2) % 2
    local, feat_dim = features.shape
    tile = tiles.shape[-1]
    rblk = local // tile
    half = local // 2
    hid = weight.shape[1]
    share = local // nrep

    def blk_swap(x, off):
        return lax.ppermute(x, "blk", [(i, i ^ off) for i in range(nblk)])

    def rep_swap(x, off):
        return lax.ppermute(x, "rep", [(i, i ^ off) for i in range(nrep)])

    def two_ways(x, off0, off1):
        return lax.ppermute(
            x,
            BOTH,
            [(b * nrep + r, (b ^ (off1 if r % 2 else off0)) * nrep + r) for b in range(nblk) for r in range(nrep)],
        )

    def one_core(x, axis, off, which):
        if axis == "blk":
            return lax.ppermute(
                x, BOTH, [(b * nrep + r, (b ^ off) * nrep + r) for b in range(nblk) for r in range(which, nrep, 2)]
            )
        return lax.ppermute(x, "rep", [(r, r ^ off) for r in range(which, nrep, 2)])

    def stage(plan):
        dealt = (len(plan),) + tiles.shape[3:]
        return pl.pallas_call(
            functools.partial(stage_kernel, rblk, plan),
            out_shape=(
                jax.ShapeDtypeStruct(dealt, tiles.dtype),
                jax.ShapeDtypeStruct(dealt, tiles.dtype),
                jax.ShapeDtypeStruct(weight.shape, weight.dtype),
                jax.ShapeDtypeStruct((1, hid), bias.dtype),
                jax.ShapeDtypeStruct(cotangent.shape, cotangent.dtype),
                jax.ShapeDtypeStruct((tile_row.shape[3], tile_row.shape[2]), jnp.int32),
            ),
            in_specs=[HBM] * 8,
            out_specs=(VMEM,) * 6,
            scratch_shapes=[
                pltpu.VMEM((1, share), label_mask.dtype),
                pltpu.VMEM(cotangent.shape, cotangent.dtype),
                pltpu.VMEM((1, 1, tile_row.shape[3], tile_row.shape[2]), jnp.int32),
                pltpu.VMEM((1, 1, tile_row.shape[3], tile_row.shape[2]), jnp.int32),
                pltpu.VMEM(tile_live.shape, jnp.int32),
                pltpu.SemaphoreType.DMA((2 * len(plan),)),
                pltpu.SemaphoreType.DMA((7,)),
            ],
            compiler_params=params(),
            cost_estimate=pl.CostEstimate(flops=0, bytes_accessed=2 * tiles.size * 2, transcendentals=0),
        )(
            tiles,
            weight,
            bias[None, :],
            label_mask[None, :],
            cotangent,
            jnp.swapaxes(tile_row, 2, 3),
            jnp.swapaxes(tile_col, 2, 3),
            tile_live,
        )

    known = [(features, 0)]
    far = nblk // 2
    while far > 4:
        known += [(blk_swap(x, far), off ^ far) for x, off in known]
        far //= 2
    plan = tuple(
        pair
        for _, base in known
        for pair in ((base ^ 4, base ^ 1), (base ^ 3, base ^ 2), (base ^ 7, base), (base ^ 6, base ^ 5))
    )
    pieces = []
    low = side == 0
    for own, base in known:
        first = two_ways(own, 4, 1)
        own_half = lax.dynamic_slice_in_dim(own, side * half, half, 0)
        second = two_ways(own_half, 3, 2)
        packed = second
        if base == 0:
            tiles_keep, tiles_send, weight_v, bias_v, masked, code = stage(plan)
            first = fence(first, second, masked)
            packed = jnp.concatenate([second, masked], axis=0)
        first_x = rep_swap(first, 1)
        third = one_core(first, "blk", 3, 0)
        across = jnp.where(core == 0, first, first_x)
        fourth = two_ways(across, 2, 1)
        packed_y = rep_swap(fence(packed, across), 2)
        if base == 0:
            tiles_x, code_x = rep_swap(fence(tiles_send, across), 1), rep_swap(fence(code, across), 1)
            other = packed_y[half:]
        second_y = packed_y[:half]
        near = jnp.concatenate([jnp.where(low, second, second_y), jnp.where(low, second_y, second)], axis=0)
        pieces += [first, near, jnp.where(core == 0, third, own), fourth]
    if npair == 2:
        cot = jnp.concatenate([jnp.where(side == 0, masked, other), jnp.where(side == 0, other, masked)], axis=0)
    else:
        stacked = jnp.stack([masked] + [rep_swap(masked, 2 * i) for i in range(1, npair)])
        order = jnp.arange(npair, dtype=jnp.int32) ^ (rep // 2)
        cot = jnp.take(stacked, order, axis=0).reshape(npair * share, hid)

    keep, send = pl.pallas_call(
        functools.partial(spmm_kernel, nrep, rblk, plan),
        out_shape=(jax.ShapeDtypeStruct((npair * share, feat_dim), jnp.float32),) * 2,
        in_specs=[SMEM] * 2 + [VMEM] * (2 + len(pieces)) + [ANY],
        out_specs=(VMEM,) * 2,
        scratch_shapes=[pltpu.VMEM(((rblk + 1) * tile, feat_dim), jnp.float32)],
        compiler_params=params(),
    )(code, code_x, tiles_keep, tiles_x, *pieces, cot)

    total, got = keep, rep_swap(send, 1)
    total = total + got
    if npair == 2:
        sent = lax.optimization_barrier((4.0 * total).astype(jnp.float16))
        total = sent.astype(jnp.float32) + rep_swap(sent, 2).astype(jnp.float32)
        total = (0.25 * total).astype(jnp.bfloat16)
    else:
        bit = 1
        while bit < npair:
            total = total + rep_swap(total, 2 * bit)
            bit *= 2
        total = total.astype(jnp.bfloat16)

    act, grads, send = pl.pallas_call(
        tail_kernel,
        out_shape=(
            jax.ShapeDtypeStruct((npair * share, hid), jnp.float32),
            jax.ShapeDtypeStruct((feat_dim // 2 + 8, hid), jnp.float32),
            jax.ShapeDtypeStruct((feat_dim // 2 + 8, hid), jnp.float32),
        ),
        in_specs=[VMEM] * 4,
        out_specs=(VMEM,) * 3,
        scratch_shapes=[pltpu.VMEM((feat_dim, hid), jnp.float32)],
        compiler_params=params(),
    )(total, weight_v, bias_v, cot)

    output = lax.dynamic_slice_in_dim(act, rep // 2 * share, share, 0).astype(jnp.bfloat16)
    grads = grads + rep_swap(send, 1)
    bit = 1
    while bit < nblk:
        grads = grads + blk_swap(grads, bit)
        bit *= 2
    grad_weight, grad_bias = pl.pallas_call(
        last_kernel,
        out_shape=(
            jax.ShapeDtypeStruct((feat_dim, hid), jnp.float32),
            jax.ShapeDtypeStruct((1, hid), jnp.float32),
        ),
        in_specs=[VMEM] * 2,
        out_specs=(VMEM,) * 2,
        compiler_params=params(),
    )(grads, rep_swap(grads, 1))
    return output, grad_weight, grad_bias.reshape(hid)


def solution(mesh):
    placed = (
        P("blk", None),
        P(),
        P(),
        P("blk", "rep", None, None, None, None),
        P("blk", "rep", None, None),
        P("blk", "rep", None, None),
        P("blk", "rep", None),
        P(BOTH),
        P(BOTH, None),
    )
    return jax.shard_map(
        shards,
        mesh=mesh,
        in_specs=placed,
        out_specs=(P(BOTH, None), P(), P()),
        check_vma=False,
    )
```

```python
import functools

import jax
import jax.numpy as jnp
from jax import lax
from jax.experimental import pallas as pl
from jax.experimental.pallas import tpu as pltpu
from jax.sharding import PartitionSpec as P

VMEM = pl.BlockSpec(memory_space=pltpu.VMEM)
SMEM = pl.BlockSpec(memory_space=pltpu.SMEM)
HBM = pl.BlockSpec(memory_space=pltpu.HBM)
ANY = pl.BlockSpec(memory_space=pl.ANY)
LIMIT = 48 * 1024 * 1024
BOTH = ("blk", "rep")


def shard_of(which, plan, j):
    return jnp.bitwise_xor(lax.axis_index("blk"), jnp.where(which == 0, plan[j][0], plan[j][1]))


def stage_kernel(rblk, plan, *refs):
    tiles_in, keep_ref, send_ref = refs[0], refs[8], refs[9]
    sources, targets = refs[1:8], refs[10:12] + refs[14:19]
    masked_ref, code_ref, tile_sems, sems = refs[12], refs[13], refs[19], refs[20]
    mask_ref, cot_ref, row_ref, col_ref, live_ref = targets[2:]
    copies = [pltpu.make_async_copy(x, y, sems.at[i]) for i, (x, y) in enumerate(zip(sources, targets))]
    core = lax.axis_index("rep") % 2
    for j in range(len(plan)):
        for i, (which, ref) in enumerate(((core, keep_ref), (1 - core, send_ref))):
            shard = shard_of(which, plan, j)
            copies.append(pltpu.make_async_copy(tiles_in.at[0, 0, shard], ref.at[j], tile_sems.at[2 * j + i]))
    for copy in copies:
        copy.start()
    for copy in copies[2:7]:
        copy.wait()
    share = cot_ref.shape[0]
    eye = lax.broadcasted_iota(jnp.int32, (share, share), 0) == lax.broadcasted_iota(jnp.int32, (share, share), 1)
    column = jnp.sum(jnp.where(eye, mask_ref[...].astype(jnp.float32), 0.0), axis=1, keepdims=True)
    masked_ref[...] = (cot_ref[...].astype(jnp.float32) * column).astype(jnp.bfloat16)
    slot = lax.broadcasted_iota(jnp.int32, code_ref.shape, 0)
    row = jnp.where(slot < live_ref[0], row_ref[0, 0], rblk)
    code_ref[...] = row * rblk + col_ref[0, 0]
    for copy in copies[:2] + copies[7:]:
        copy.wait()


def spmm_kernel(nrep, rblk, plan, *refs):
    codes, tiles = refs[:2], refs[2:4]
    pieces = refs[4 : 4 + len(plan)]
    keep_ref, send_ref, acc = refs[5 + len(plan) :]
    core = lax.axis_index("rep") % 2
    npair = nrep // 2
    slots, tile = tiles[0].shape[1], tiles[0].shape[2]

    acc[...] = jnp.zeros_like(acc)
    for j, piece in enumerate(pieces):
        shard = shard_of(core, plan, j)
        for code_ref, tiles_ref in zip(codes, tiles):
            for k in range(slots):
                code = code_ref[k, shard]
                row, col = code // rblk, code % rblk
                block = piece[pl.ds(pl.multiple_of(col * tile, tile), tile)]
                prod = jnp.dot(tiles_ref[j, k], block, preferred_element_type=jnp.float32)
                at = pl.ds(pl.multiple_of(row * tile, tile), tile)
                acc[at] = acc[at] + prod

    share = rblk * tile // nrep

    def part(owner):
        return acc[pl.ds(pl.multiple_of(owner * share, share), share)]

    for p in range(npair):
        keep_ref[pl.ds(p * share, share)] = part(2 * p + core)
        send_ref[pl.ds(p * share, share)] = part(2 * p + 1 - core)


def tail_kernel(*refs):
    agg_ref, weight_ref, bias_ref, cot_ref, act_ref, keep_ref, send_ref, grad = refs
    agg = agg_ref[...]
    pre = jnp.dot(agg, weight_ref[...], preferred_element_type=jnp.float32) + bias_ref[...]
    sigma = 1.0 / (1.0 + jnp.exp(-pre))
    act_ref[...] = pre * sigma
    delta = cot_ref[...].astype(jnp.float32) * (sigma * (1.0 + pre * (1.0 - sigma)))
    gw = lax.dot_general(
        agg, delta.astype(jnp.bfloat16), (((0,), (0,)), ((), ())), preferred_element_type=jnp.float32
    )
    gb = jnp.sum(delta, axis=0, keepdims=True)
    half = gw.shape[0] // 2
    core = lax.axis_index("rep") % 2
    grad[...] = gw
    for ref, which in ((keep_ref, core), (send_ref, 1 - core)):
        ref[pl.ds(0, half)] = grad[pl.ds(pl.multiple_of(which * half, half), half)]
        ref[pl.ds(half, 8)] = jnp.broadcast_to(gb, (8, gb.shape[1]))


def last_kernel(mine_ref, other_ref, gw_ref, gb_ref):
    half = gw_ref.shape[0] // 2
    core = lax.axis_index("rep") % 2
    gw_ref[pl.ds(pl.multiple_of(core * half, half), half)] = mine_ref[pl.ds(0, half)]
    gw_ref[pl.ds(pl.multiple_of((1 - core) * half, half), half)] = other_ref[pl.ds(0, half)]
    gb_ref[...] = jnp.where(core == 0, mine_ref[pl.ds(half, 1)], other_ref[pl.ds(half, 1)])


def fence_kernel(x_ref, *refs):
    refs[-1][...] = x_ref[...]


def fence(x, *others):
    return pl.pallas_call(
        fence_kernel,
        out_shape=jax.ShapeDtypeStruct(x.shape, x.dtype),
        in_specs=[VMEM] + [ANY] * len(others),
        out_specs=VMEM,
        compiler_params=params(),
    )(x, *others)


def params():
    return pltpu.CompilerParams(vmem_limit_bytes=LIMIT)


def shards(features, weight, bias, tiles, tile_row, tile_col, tile_live, label_mask, cotangent):
    nblk, nrep = lax.axis_size("blk"), lax.axis_size("rep")
    npair = nrep // 2
    rep = lax.axis_index("rep")
    core = rep % 2
    side = (rep // 2) % 2
    local, feat_dim = features.shape
    tile = tiles.shape[-1]
    rblk = local // tile
    half = local // 2
    hid = weight.shape[1]
    share = local // nrep

    def blk_swap(x, off):
        return lax.ppermute(x, "blk", [(i, i ^ off) for i in range(nblk)])

    def rep_swap(x, off):
        return lax.ppermute(x, "rep", [(i, i ^ off) for i in range(nrep)])

    def two_ways(x, off0, off1):
        return lax.ppermute(
            x,
            BOTH,
            [(b * nrep + r, (b ^ (off1 if r % 2 else off0)) * nrep + r) for b in range(nblk) for r in range(nrep)],
        )

    def one_core(x, axis, off, which):
        if axis == "blk":
            return lax.ppermute(
                x, BOTH, [(b * nrep + r, (b ^ off) * nrep + r) for b in range(nblk) for r in range(which, nrep, 2)]
            )
        return lax.ppermute(x, "rep", [(r, r ^ off) for r in range(which, nrep, 2)])

    def stage(plan):
        dealt = (len(plan),) + tiles.shape[3:]
        return pl.pallas_call(
            functools.partial(stage_kernel, rblk, plan),
            out_shape=(
                jax.ShapeDtypeStruct(dealt, tiles.dtype),
                jax.ShapeDtypeStruct(dealt, tiles.dtype),
                jax.ShapeDtypeStruct(weight.shape, weight.dtype),
                jax.ShapeDtypeStruct((1, hid), bias.dtype),
                jax.ShapeDtypeStruct(cotangent.shape, cotangent.dtype),
                jax.ShapeDtypeStruct((tile_row.shape[3], tile_row.shape[2]), jnp.int32),
            ),
            in_specs=[HBM] * 8,
            out_specs=(VMEM,) * 6,
            scratch_shapes=[
                pltpu.VMEM((1, share), label_mask.dtype),
                pltpu.VMEM(cotangent.shape, cotangent.dtype),
                pltpu.VMEM((1, 1, tile_row.shape[3], tile_row.shape[2]), jnp.int32),
                pltpu.VMEM((1, 1, tile_row.shape[3], tile_row.shape[2]), jnp.int32),
                pltpu.VMEM(tile_live.shape, jnp.int32),
                pltpu.SemaphoreType.DMA((2 * len(plan),)),
                pltpu.SemaphoreType.DMA((7,)),
            ],
            compiler_params=params(),
            cost_estimate=pl.CostEstimate(flops=0, bytes_accessed=2 * tiles.size * 2, transcendentals=0),
        )(
            tiles,
            weight,
            bias[None, :],
            label_mask[None, :],
            cotangent,
            jnp.swapaxes(tile_row, 2, 3),
            jnp.swapaxes(tile_col, 2, 3),
            tile_live,
        )

    known = [(features, 0)]
    far = nblk // 2
    while far > 4:
        known += [(blk_swap(x, far), off ^ far) for x, off in known]
        far //= 2
    plan = tuple(
        pair
        for _, base in known
        for pair in ((base ^ 4, base ^ 1), (base ^ 3, base ^ 2), (base ^ 7, base), (base ^ 6, base ^ 5))
    )
    pieces = []
    low = side == 0
    for own, base in known:
        first = two_ways(own, 4, 1)
        own_half = lax.dynamic_slice_in_dim(own, side * half, half, 0)
        second = two_ways(own_half, 3, 2)
        packed = second
        if base == 0:
            tiles_keep, tiles_send, weight_v, bias_v, masked, code = stage(plan)
            first = fence(first, second, masked)
            packed = jnp.concatenate([second, masked], axis=0)
        first_x = rep_swap(first, 1)
        third = one_core(first, "blk", 3, 0)
        across = jnp.where(core == 0, first, first_x)
        fourth = two_ways(across, 2, 1)
        packed_y = rep_swap(fence(packed, across), 2)
        if base == 0:
            tiles_x, code_x = rep_swap(fence(tiles_send, across), 1), rep_swap(fence(code, across), 1)
            other = packed_y[half:]
        second_y = packed_y[:half]
        near = jnp.concatenate([jnp.where(low, second, second_y), jnp.where(low, second_y, second)], axis=0)
        pieces += [first, near, jnp.where(core == 0, third, own), fourth]
    if npair == 2:
        cot = jnp.concatenate([jnp.where(side == 0, masked, other), jnp.where(side == 0, other, masked)], axis=0)
    else:
        stacked = jnp.stack([masked] + [rep_swap(masked, 2 * i) for i in range(1, npair)])
        order = jnp.arange(npair, dtype=jnp.int32) ^ (rep // 2)
        cot = jnp.take(stacked, order, axis=0).reshape(npair * share, hid)

    keep, send = pl.pallas_call(
        functools.partial(spmm_kernel, nrep, rblk, plan),
        out_shape=(jax.ShapeDtypeStruct((npair * share, feat_dim), jnp.float32),) * 2,
        in_specs=[SMEM] * 2 + [VMEM] * (2 + len(pieces)) + [ANY],
        out_specs=(VMEM,) * 2,
        scratch_shapes=[pltpu.VMEM(((rblk + 1) * tile, feat_dim), jnp.float32)],
        compiler_params=params(),
    )(code, code_x, tiles_keep, tiles_x, *pieces, cot)

    total, got = keep, rep_swap(send, 1)
    total = total + got
    if npair == 2:
        sent = lax.optimization_barrier((4.0 * total).astype(jnp.float16))
        total = sent.astype(jnp.float32) + rep_swap(sent, 2).astype(jnp.float32)
        total = (0.25 * total).astype(jnp.bfloat16)
    else:
        bit = 1
        while bit < npair:
            total = total + rep_swap(total, 2 * bit)
            bit *= 2
        total = total.astype(jnp.bfloat16)

    act, grads, send = pl.pallas_call(
        tail_kernel,
        out_shape=(
            jax.ShapeDtypeStruct((npair * share, hid), jnp.float32),
            jax.ShapeDtypeStruct((feat_dim // 2 + 8, hid), jnp.float32),
            jax.ShapeDtypeStruct((feat_dim // 2 + 8, hid), jnp.float32),
        ),
        in_specs=[VMEM] * 4,
        out_specs=(VMEM,) * 3,
        scratch_shapes=[pltpu.VMEM((feat_dim, hid), jnp.float32)],
        compiler_params=params(),
    )(total, weight_v, bias_v, cot)

    output = lax.dynamic_slice_in_dim(act, rep // 2 * share, share, 0).astype(jnp.bfloat16)
    grads = grads + rep_swap(send, 1)
    bits = [1 << i for i in range(nblk.bit_length() - 1)]
    for bit0, bit1 in zip(bits, bits[1:] + bits[:1]):
        grads = grads + two_ways(grads, bit0, bit1)
    grad_weight, grad_bias = pl.pallas_call(
        last_kernel,
        out_shape=(
            jax.ShapeDtypeStruct((feat_dim, hid), jnp.float32),
            jax.ShapeDtypeStruct((1, hid), jnp.float32),
        ),
        in_specs=[VMEM] * 2,
        out_specs=(VMEM,) * 2,
        compiler_params=params(),
    )(grads, rep_swap(grads, 1))
    return output, grad_weight, grad_bias.reshape(hid)


def solution(mesh):
    placed = (
        P("blk", None),
        P(),
        P(),
        P("blk", "rep", None, None, None, None),
        P("blk", "rep", None, None),
        P("blk", "rep", None, None),
        P("blk", "rep", None),
        P(BOTH),
        P(BOTH, None),
    )
    return jax.shard_map(
        shards,
        mesh=mesh,
        in_specs=placed,
        out_specs=(P(BOTH, None), P(), P()),
        check_vma=False,
    )
```

```python
import functools

import jax
import jax.numpy as jnp
from jax import lax
from jax.experimental import pallas as pl
from jax.experimental.pallas import tpu as pltpu
from jax.sharding import PartitionSpec as P

VMEM = pl.BlockSpec(memory_space=pltpu.VMEM)
SMEM = pl.BlockSpec(memory_space=pltpu.SMEM)
HBM = pl.BlockSpec(memory_space=pltpu.HBM)
ANY = pl.BlockSpec(memory_space=pl.ANY)
LIMIT = 48 * 1024 * 1024
BOTH = ("blk", "rep")


def shard_of(which, plan, j):
    return jnp.bitwise_xor(lax.axis_index("blk"), jnp.where(which == 0, plan[j][0], plan[j][1]))


def stage_kernel(rblk, plan, *refs):
    tiles_in, keep_ref, send_ref = refs[0], refs[8], refs[9]
    sources, targets = refs[1:8], refs[10:12] + refs[14:19]
    masked_ref, code_ref, tile_sems, sems = refs[12], refs[13], refs[19], refs[20]
    mask_ref, cot_ref, row_ref, col_ref, live_ref = targets[2:]
    copies = [pltpu.make_async_copy(x, y, sems.at[i]) for i, (x, y) in enumerate(zip(sources, targets))]
    core = lax.axis_index("rep") % 2
    for j in range(len(plan)):
        for i, (which, ref) in enumerate(((core, keep_ref), (1 - core, send_ref))):
            shard = shard_of(which, plan, j)
            copies.append(pltpu.make_async_copy(tiles_in.at[0, 0, shard], ref.at[j], tile_sems.at[2 * j + i]))
    for copy in copies:
        copy.start()
    for copy in copies[2:7]:
        copy.wait()
    share = cot_ref.shape[0]
    eye = lax.broadcasted_iota(jnp.int32, (share, share), 0) == lax.broadcasted_iota(jnp.int32, (share, share), 1)
    column = jnp.sum(jnp.where(eye, mask_ref[...].astype(jnp.float32), 0.0), axis=1, keepdims=True)
    masked_ref[...] = (cot_ref[...].astype(jnp.float32) * column).astype(jnp.bfloat16)
    slot = lax.broadcasted_iota(jnp.int32, code_ref.shape, 0)
    row = jnp.where(slot < live_ref[0], row_ref[0, 0], rblk)
    code_ref[...] = row * rblk + col_ref[0, 0]
    for copy in copies[:2] + copies[7:]:
        copy.wait()


def spmm_kernel(nrep, rblk, plan, *refs):
    codes, tiles = refs[:2], refs[2:4]
    pieces = refs[4 : 4 + len(plan)]
    keep_ref, send_ref, acc = refs[5 + len(plan) :]
    core = lax.axis_index("rep") % 2
    npair = nrep // 2
    slots, tile = tiles[0].shape[1], tiles[0].shape[2]

    acc[...] = jnp.zeros_like(acc)
    for j, piece in enumerate(pieces):
        shard = shard_of(core, plan, j)
        for code_ref, tiles_ref in zip(codes, tiles):
            for k in range(slots):
                code = code_ref[k, shard]
                row, col = code // rblk, code % rblk
                block = piece[pl.ds(pl.multiple_of(col * tile, tile), tile)]
                prod = jnp.dot(tiles_ref[j, k], block, preferred_element_type=jnp.float32)
                at = pl.ds(pl.multiple_of(row * tile, tile), tile)
                acc[at] = acc[at] + prod

    share = rblk * tile // nrep

    def part(owner):
        return acc[pl.ds(pl.multiple_of(owner * share, share), share)]

    for p in range(npair):
        keep_ref[pl.ds(p * share, share)] = part(2 * p + core)
        send_ref[pl.ds(p * share, share)] = part(2 * p + 1 - core)


def tail_kernel(*refs):
    agg_ref, weight_ref, bias_ref, cot_ref, act_ref, keep_ref, send_ref, grad = refs
    agg = agg_ref[...]
    pre = jnp.dot(agg, weight_ref[...], preferred_element_type=jnp.float32) + bias_ref[...]
    sigma = 1.0 / (1.0 + jnp.exp(-pre))
    act_ref[...] = pre * sigma
    delta = cot_ref[...].astype(jnp.float32) * (sigma * (1.0 + pre * (1.0 - sigma)))
    gw = lax.dot_general(
        agg, delta.astype(jnp.bfloat16), (((0,), (0,)), ((), ())), preferred_element_type=jnp.float32
    )
    gb = jnp.sum(delta, axis=0, keepdims=True)
    half = gw.shape[0] // 2
    core = lax.axis_index("rep") % 2
    grad[...] = gw
    for ref, which in ((keep_ref, core), (send_ref, 1 - core)):
        ref[pl.ds(0, half)] = grad[pl.ds(pl.multiple_of(which * half, half), half)]
        ref[pl.ds(half, 8)] = jnp.broadcast_to(gb, (8, gb.shape[1]))


def last_kernel(mine_ref, other_ref, gw_ref, gb_ref):
    half = gw_ref.shape[0] // 2
    core = lax.axis_index("rep") % 2
    gw_ref[pl.ds(pl.multiple_of(core * half, half), half)] = mine_ref[pl.ds(0, half)]
    gw_ref[pl.ds(pl.multiple_of((1 - core) * half, half), half)] = other_ref[pl.ds(0, half)]
    gb_ref[...] = mine_ref[pl.ds(half, 1)]


def fence_kernel(x_ref, *refs):
    refs[-1][...] = x_ref[...]


def fence(x, *others):
    return pl.pallas_call(
        fence_kernel,
        out_shape=jax.ShapeDtypeStruct(x.shape, x.dtype),
        in_specs=[VMEM] + [ANY] * len(others),
        out_specs=VMEM,
        compiler_params=params(),
    )(x, *others)


def params():
    return pltpu.CompilerParams(vmem_limit_bytes=LIMIT)


def shards(features, weight, bias, tiles, tile_row, tile_col, tile_live, label_mask, cotangent):
    nblk, nrep = lax.axis_size("blk"), lax.axis_size("rep")
    npair = nrep // 2
    rep = lax.axis_index("rep")
    core = rep % 2
    side = (rep // 2) % 2
    local, feat_dim = features.shape
    tile = tiles.shape[-1]
    rblk = local // tile
    half = local // 2
    hid = weight.shape[1]
    share = local // nrep

    def blk_swap(x, off):
        return lax.ppermute(x, "blk", [(i, i ^ off) for i in range(nblk)])

    def rep_swap(x, off):
        return lax.ppermute(x, "rep", [(i, i ^ off) for i in range(nrep)])

    def two_ways(x, off0, off1):
        return lax.ppermute(
            x,
            BOTH,
            [(b * nrep + r, (b ^ (off1 if r % 2 else off0)) * nrep + r) for b in range(nblk) for r in range(nrep)],
        )

    def one_core(x, axis, off, which):
        if axis == "blk":
            return lax.ppermute(
                x, BOTH, [(b * nrep + r, (b ^ off) * nrep + r) for b in range(nblk) for r in range(which, nrep, 2)]
            )
        return lax.ppermute(x, "rep", [(r, r ^ off) for r in range(which, nrep, 2)])

    def stage(plan):
        dealt = (len(plan),) + tiles.shape[3:]
        return pl.pallas_call(
            functools.partial(stage_kernel, rblk, plan),
            out_shape=(
                jax.ShapeDtypeStruct(dealt, tiles.dtype),
                jax.ShapeDtypeStruct(dealt, tiles.dtype),
                jax.ShapeDtypeStruct(weight.shape, weight.dtype),
                jax.ShapeDtypeStruct((1, hid), bias.dtype),
                jax.ShapeDtypeStruct(cotangent.shape, cotangent.dtype),
                jax.ShapeDtypeStruct((tile_row.shape[3], tile_row.shape[2]), jnp.int32),
            ),
            in_specs=[HBM] * 8,
            out_specs=(VMEM,) * 6,
            scratch_shapes=[
                pltpu.VMEM((1, share), label_mask.dtype),
                pltpu.VMEM(cotangent.shape, cotangent.dtype),
                pltpu.VMEM((1, 1, tile_row.shape[3], tile_row.shape[2]), jnp.int32),
                pltpu.VMEM((1, 1, tile_row.shape[3], tile_row.shape[2]), jnp.int32),
                pltpu.VMEM(tile_live.shape, jnp.int32),
                pltpu.SemaphoreType.DMA((2 * len(plan),)),
                pltpu.SemaphoreType.DMA((7,)),
            ],
            compiler_params=params(),
            cost_estimate=pl.CostEstimate(flops=0, bytes_accessed=2 * tiles.size * 2, transcendentals=0),
        )(
            tiles,
            weight,
            bias[None, :],
            label_mask[None, :],
            cotangent,
            jnp.swapaxes(tile_row, 2, 3),
            jnp.swapaxes(tile_col, 2, 3),
            tile_live,
        )

    known = [(features, 0)]
    far = nblk // 2
    while far > 4:
        known += [(blk_swap(x, far), off ^ far) for x, off in known]
        far //= 2
    plan = tuple(
        pair
        for _, base in known
        for pair in ((base ^ 4, base ^ 1), (base ^ 3, base ^ 2), (base ^ 7, base), (base ^ 6, base ^ 5))
    )
    pieces = []
    low = side == 0
    for own, base in known:
        first = two_ways(own, 4, 1)
        own_half = lax.dynamic_slice_in_dim(own, side * half, half, 0)
        second = two_ways(own_half, 3, 2)
        packed = second
        if base == 0:
            tiles_keep, tiles_send, weight_v, bias_v, masked, code = stage(plan)
            first = fence(first, second, masked)
            packed = jnp.concatenate([second, masked], axis=0)
        first_x = rep_swap(first, 1)
        third = one_core(first, "blk", 3, 0)
        across = jnp.where(core == 0, first, first_x)
        fourth = two_ways(across, 2, 1)
        packed_y = rep_swap(fence(packed, across), 2)
        if base == 0:
            tiles_x, code_x = rep_swap(fence(tiles_send, across), 1), rep_swap(fence(code, across), 1)
            other = packed_y[half:]
        second_y = packed_y[:half]
        near = jnp.concatenate([jnp.where(low, second, second_y), jnp.where(low, second_y, second)], axis=0)
        pieces += [first, near, jnp.where(core == 0, third, own), fourth]
    if npair == 2:
        cot = jnp.concatenate([jnp.where(side == 0, masked, other), jnp.where(side == 0, other, masked)], axis=0)
    else:
        stacked = jnp.stack([masked] + [rep_swap(masked, 2 * i) for i in range(1, npair)])
        order = jnp.arange(npair, dtype=jnp.int32) ^ (rep // 2)
        cot = jnp.take(stacked, order, axis=0).reshape(npair * share, hid)

    keep, send = pl.pallas_call(
        functools.partial(spmm_kernel, nrep, rblk, plan),
        out_shape=(jax.ShapeDtypeStruct((npair * share, feat_dim), jnp.float32),) * 2,
        in_specs=[SMEM] * 2 + [VMEM] * (2 + len(pieces)) + [ANY],
        out_specs=(VMEM,) * 2,
        scratch_shapes=[pltpu.VMEM(((rblk + 1) * tile, feat_dim), jnp.float32)],
        compiler_params=params(),
    )(code, code_x, tiles_keep, tiles_x, *pieces, cot)

    total, got = keep, 0.25 * rep_swap((4.0 * send).astype(jnp.float16), 1).astype(jnp.float32)
    total = total + got
    if npair == 2:
        sent = lax.optimization_barrier((4.0 * total).astype(jnp.float16))
        total = sent.astype(jnp.float32) + rep_swap(sent, 2).astype(jnp.float32)
        total = (0.25 * total).astype(jnp.bfloat16)
    else:
        bit = 1
        while bit < npair:
            total = total + rep_swap(total, 2 * bit)
            bit *= 2
        total = total.astype(jnp.bfloat16)

    act, grads, send = pl.pallas_call(
        tail_kernel,
        out_shape=(
            jax.ShapeDtypeStruct((npair * share, hid), jnp.float32),
            jax.ShapeDtypeStruct((feat_dim // 2 + 8, hid), jnp.float32),
            jax.ShapeDtypeStruct((feat_dim // 2 + 8, hid), jnp.float32),
        ),
        in_specs=[VMEM] * 4,
        out_specs=(VMEM,) * 3,
        scratch_shapes=[pltpu.VMEM((feat_dim, hid), jnp.float32)],
        compiler_params=params(),
    )(total, weight_v, bias_v, cot)

    output = lax.dynamic_slice_in_dim(act, rep // 2 * share, share, 0).astype(jnp.bfloat16)
    grads = grads + rep_swap(send, 1)
    bit = 1
    while bit < nblk:
        grads = grads + blk_swap(grads, bit)
        bit *= 2
    grad_weight, grad_bias = pl.pallas_call(
        last_kernel,
        out_shape=(
            jax.ShapeDtypeStruct((feat_dim, hid), jnp.float32),
            jax.ShapeDtypeStruct((1, hid), jnp.float32),
        ),
        in_specs=[VMEM] * 2,
        out_specs=(VMEM,) * 2,
        compiler_params=params(),
    )(grads, rep_swap(grads, 1))
    return output, grad_weight, grad_bias.reshape(hid)


def solution(mesh):
    placed = (
        P("blk", None),
        P(),
        P(),
        P("blk", "rep", None, None, None, None),
        P("blk", "rep", None, None),
        P("blk", "rep", None, None),
        P("blk", "rep", None),
        P(BOTH),
        P(BOTH, None),
    )
    return jax.shard_map(
        shards,
        mesh=mesh,
        in_specs=placed,
        out_specs=(P(BOTH, None), P(), P()),
        check_vma=False,
    )
```
